32 devices in a mesh: leaf: 4 (over x, core), front: 8 (over z, y).
Axes of the slice: x: 2, y: 2, z: 4, core: 2. Of those that a mesh axis runs over, the one named last changes fastest.
Arguments:
- front_matrix: float32 [4, 2048, 2048], P('leaf', 'front'), as said below
- child_blocks: float32 [32, 4, 3, 128, 128], P(('leaf', 'front')), may hold values from -0.046875 to 0.046875
- child_target: int32 [32, 4, 3], P(('leaf', 'front')), may hold values from 0 to 31, as said below
- child_count: int32 [32, 4], P(('leaf', 'front')), may hold values from 1 to 3, as said below
- shot_rhs: float32 [4, 64, 2048], P('leaf'), may hold values from -6 to 6
Outputs:
- factored: float32 [4, 2048, 2048], P('leaf', 'front')
- eliminated: float32 [4, 64, 2048], P('leaf')
The draws below stay inside these ranges and needn't reach their ends.
Inputs may be any that keep to these rules, and one draw needn't show every extreme that they name: `child_target`: A bucket's code places its block on a row block that the receiving device (leaf index of the bucket, front index of the sender) holds, at a column block no later than that row block. Slots from child_count on are empty and hold no data. In every draw some leaf index receives 3 live blocks from every sender. `front_matrix`: after the child blocks are added, the symmetric matrix that each front's lower triangle defines is positive definite.
All inputs are finite; a program needn't handle non-finite values.
Results may differ from the reference program's by a relative error of at most 0.00013.
Values sent between devices are 32-bit elements; how exact they have to be, the bound alone decides.
A program may use at most 64 MiB of HBM per device.

```python
import jax
import jax.numpy as jnp
from jax import lax

BLOCK = 128
ORDER = 2048
PIVOTS = 1024
NRHS = 64
FR_DEV = 1
CAP = 3
FRONTS = 4
SENDERS = 32
NCB = 16
RB_LOC = 2
N_LEAF = 4
N_FRONT = 8


def draw_front_matrix(key, part):
    key_off, key_diag = jax.random.split(key)
    array_shape = (FRONTS, ORDER, ORDER)
    offdiag = jax.random.normal(key_off, array_shape, jnp.float32)
    offdiag = offdiag * (0.2 * ORDER ** (-0.5))
    row_ids = lax.broadcasted_iota(jnp.int32, (ORDER, ORDER), 0)
    col_ids = lax.broadcasted_iota(jnp.int32, (ORDER, ORDER), 1)
    distance = jnp.abs(row_ids - col_ids)
    coupling = jnp.where((distance == 1) | (distance == 32), jnp.float32(-1.0), jnp.float32(0.0))
    identity_mat = jnp.where(distance == 0, jnp.float32(1.0), jnp.float32(0.0))
    diagonal = jax.random.uniform(key_diag, (FRONTS, ORDER), jnp.float32, 5.5, 6.5)
    return offdiag * (1.0 - identity_mat) + coupling[None, :, :] + diagonal[:, :, None] * identity_mat


def draw_child_target(key, part):
    key_front, key_row, key_col = jax.random.split(key, 3)
    target_dims = (SENDERS, N_LEAF, CAP)
    front_pick = jax.random.randint(key_front, target_dims, 0, FR_DEV)
    row_pick = jax.random.randint(key_row, target_dims, 0, RB_LOC)
    sender_front = lax.broadcasted_iota(jnp.int32, target_dims, 0) % N_FRONT
    global_row = sender_front * RB_LOC + row_pick
    col_pick = jax.random.randint(key_col, target_dims, 0, global_row + 1)
    return ((front_pick * RB_LOC + row_pick) * NCB + col_pick).astype(jnp.int32)


def draw_child_count(key, part):
    key_count, key_full = jax.random.split(key)
    counts = jax.random.randint(key_count, (SENDERS, N_LEAF), 1, CAP + 1)
    full_leaf = jax.random.randint(key_full, (), 0, N_LEAF)
    column_ids = lax.broadcasted_iota(jnp.int32, (SENDERS, N_LEAF), 1)
    return jnp.where(column_ids == full_leaf, CAP, counts).astype(jnp.int32)


def block_scale(stream_key, shape, cuts, low, largest):
    def one(dim, shards_of):
        steps = jax.random.uniform(jax.random.fold_in(jax.random.fold_in(stream_key, 6), dim), (shards_of,), jnp.float32, low / len(cuts), largest / len(cuts))
        return jnp.repeat(jnp.exp(steps), shape[dim] // shards_of).reshape((-1,) + (1,) * (len(shape) - dim - 1))

    level = one(*cuts[0])
    for cut in cuts[1:]:
        level = level * one(*cut)
    return level


def scatter_about(stream_key, extent, scale, limit, shards=(), kind=jnp.bfloat16):
    factor_of = block_scale(stream_key, extent, shards, -0.22, 0.18) if shards else 1.0
    result = jax.random.normal(stream_key, extent, jnp.float32) * scale * factor_of
    return jnp.minimum(jnp.maximum(result, -limit), limit).astype(kind)


def setup_inputs(seed: int = 0) -> dict:
    keys = jax.random.split(jax.random.key(seed), 6)
    front_matrix = draw_front_matrix(jax.random.fold_in(keys[5], 71), 0)
    child_blocks = scatter_about(keys[1], (SENDERS, N_LEAF, CAP, BLOCK, BLOCK), (0.15 * ORDER ** -0.5), 0.046875, ((0, 32),), jnp.float32)
    child_target = draw_child_target(jax.random.fold_in(keys[5], 71), 0)
    child_count = draw_child_count(jax.random.fold_in(keys[5], 71), 0)
    shot_rhs = scatter_about(keys[4], (FRONTS, NRHS, ORDER), 1.0, 6.0, ((0, 4),), jnp.float32)
    return {"front_matrix": front_matrix, "child_blocks": child_blocks, "child_target": child_target, "child_count": child_count, "shot_rhs": shot_rhs}


def lower_sym(square):
    return jnp.tril(square) + jnp.swapaxes(jnp.tril(square, -1), -1, -2)

def extend_add(child_blocks, child_target, child_count):
    slot_ids = lax.broadcasted_iota(jnp.int32, child_target.shape, 2)
    sender_ids = lax.broadcasted_iota(jnp.int32, child_target.shape, 0)
    dest_leaf = lax.broadcasted_iota(jnp.int32, child_target.shape, 1)
    live_mask = slot_ids < child_count[:, :, None]
    front_ids = dest_leaf * FR_DEV + child_target // (RB_LOC * NCB)
    row_ids = sender_ids % N_FRONT * RB_LOC + child_target // NCB % RB_LOC
    col_ids = child_target % NCB
    values = jnp.where(live_mask[:, :, :, None, None], child_blocks, jnp.float32(0.0))
    block_grid = jnp.zeros((FRONTS, NCB, NCB, BLOCK, BLOCK), jnp.float32)
    block_grid = block_grid.at[front_ids, row_ids, col_ids].add(values)
    return block_grid.transpose(0, 1, 3, 2, 4).reshape(FRONTS, ORDER, ORDER)

def factor_one(operands):
    matrix, current_rhs = operands
    row_index = jnp.arange(ORDER, dtype=jnp.int32)[:, None]
    col_index = jnp.arange(ORDER, dtype=jnp.int32)[None, :]
    left_parts = []
    diag_parts = []
    solved_parts = []
    for pivot_step in range(PIVOTS // BLOCK):
        start_col = pivot_step * BLOCK
        end_col = start_col + BLOCK
        column_panel = matrix[:, start_col:end_col]
        pivot_factor = jnp.linalg.cholesky(lower_sym(column_panel[start_col:end_col]))
        panel_solved = jax.scipy.linalg.solve_triangular(pivot_factor, column_panel.T, lower=True).T
        panel_solved = jnp.where(row_index < start_col, jnp.float32(0.0), panel_solved)
        panel_solved = panel_solved.at[start_col:end_col].set(pivot_factor)
        tail_panel = panel_solved[end_col:]
        update = jnp.dot(panel_solved.astype(jnp.float32), tail_panel.T.astype(jnp.float32), precision=lax.Precision.HIGHEST, preferred_element_type=jnp.float32)
        matrix = matrix.at[:, end_col:].add(-update)
        zeta = jax.scipy.linalg.solve_triangular(pivot_factor, current_rhs[:, start_col:end_col].T, lower=True).T
        rhs_update = jnp.dot(zeta.astype(jnp.float32), tail_panel.T.astype(jnp.float32), precision=lax.Precision.HIGHEST, preferred_element_type=jnp.float32)
        current_rhs = current_rhs.at[:, end_col:].add(-rhs_update)
        pivots_now = jnp.diagonal(pivot_factor)
        left_parts.append(panel_solved / pivots_now[None, :])
        diag_parts.append(pivots_now * pivots_now)
        solved_parts.append(zeta * pivots_now[None, :])
    combined = jnp.concatenate(left_parts + [matrix[:, PIVOTS:]], axis=1)
    combined = jnp.where(row_index < col_index, jnp.float32(0.0), combined)
    diag_full = jnp.concatenate(diag_parts + [jnp.zeros((ORDER - PIVOTS,), jnp.float32)], axis=0)
    on_diagonal = (row_index == col_index) & (col_index < PIVOTS)
    factored = jnp.where(on_diagonal, diag_full[None, :], combined)
    eliminated = jnp.concatenate(solved_parts + [current_rhs[:, PIVOTS:]], axis=1)
    return (factored, eliminated)

def reference(front_matrix, child_blocks, child_target, child_count, shot_rhs):
    assembled = front_matrix + extend_add(child_blocks, child_target, child_count)
    factored, eliminated = lax.map(factor_one, (assembled, shot_rhs))
    return (factored, eliminated)
```

```python
import functools

import jax
import jax.numpy as jnp
from jax import lax
from jax.experimental import pallas as pl
from jax.experimental.pallas import tpu as pltpu
from jax.sharding import PartitionSpec as P

BLOCK = 128
PIVOTS = 1024
STEPS = PIVOTS // BLOCK
PANEL = 8
MESH = pl.DeviceIdType.MESH
NT = (((1,), (1,)), ((), ()))
TN = (((0,), (0,)), ((), ()))


def split(value):
    high = value.astype(jnp.bfloat16)
    low = (value - high.astype(jnp.float32)).astype(jnp.bfloat16)
    return high, low


def dot3(left, right):
    dot = functools.partial(lax.dot_general, dimension_numbers=NT, preferred_element_type=jnp.float32)
    return dot(left[0], right[0]) + (dot(left[0], right[1]) + dot(left[1], right[0]))


def panel_factor(panel, start):
    lead = pltpu.roll(panel[:, :BLOCK], lax.rem(BLOCK - start, BLOCK), 1)
    full = (PANEL, BLOCK)
    entry = [[jnp.broadcast_to(lead[i : i + 1, j : j + 1], full) for j in range(i + 1)] for i in range(PANEL)]
    lower = [[None] * PANEL for _ in range(PANEL)]
    for j in range(PANEL):
        inverse = 1.0 / entry[j][j]
        for i in range(j + 1, PANEL):
            lower[i][j] = entry[i][j] * inverse
        for i in range(j + 1, PANEL):
            for k in range(j + 1, i + 1):
                entry[i][k] = entry[i][k] - lower[i][j] * entry[k][j]
    rows = lax.broadcasted_iota(jnp.int32, full, 0)
    inverse = [[None] * PANEL for _ in range(PANEL)]
    left, right = panel[:, :BLOCK], panel[:, BLOCK:]
    new_left, new_right = left, right
    for j in range(PANEL):
        column = jnp.zeros(full, jnp.float32)
        for i in range(j + 1, PANEL):
            total = lower[i][j]
            for k in range(j + 1, i):
                total = total + lower[i][k] * inverse[k][j]
            inverse[i][j] = -total
            column = jnp.where(rows == i, -total, column)
        if j < PANEL - 1:
            new_left = new_left + column * left[j : j + 1]
            new_right = new_right + column * right[j : j + 1]
    pivots = entry[0][0]
    for i in range(1, PANEL):
        pivots = jnp.where(rows == i, entry[i][i], pivots)
    return new_left, new_right, pivots


def block_factor(work):
    def body(index, carry):
        start = pl.multiple_of(index * PANEL, PANEL)
        left, right, pivots = panel_factor(work[pl.ds(start, PANEL), :], start)
        work[pl.ds(start, PANEL), :BLOCK] = left
        work[pl.ds(start, PANEL), BLOCK:] = right
        lanes = lax.broadcasted_iota(jnp.int32, left.shape, 1)
        scaled = jnp.where(lanes >= start + PANEL, left / pivots, 0.0)
        both = jnp.concatenate([left, right], axis=1)
        work[...] -= lax.dot_general(
            scaled, both, TN, precision=lax.Precision.HIGHEST, preferred_element_type=jnp.float32
        )
        return carry

    lax.fori_loop(0, BLOCK // PANEL, body, 0)


def kernel(
    leafs, fronts, front, child, codes, rhs, out, elim,
    child_in, codes_in, mine, top, high, low, lead, work, own_w, far_w, tail_out, tail_in,
    child_send, child_recv, code_send, code_recv, top_send, top_recv, relay_send,
    far_send, far_recv, tail_send, tail_recv,
):
    rows, order = front.shape
    shots = rhs.shape[0]
    slots = child.shape[1]
    col_blocks = order // BLOCK
    row_blocks = rows // BLOCK
    tops = PIVOTS // rows
    slab = fronts // 4
    me = lax.axis_index("front")
    leaf = lax.axis_index("leaf")
    depth = me // slab
    here = me < tops
    below = me >= tops

    def to(front_id):
        return {"front": front_id}

    def remote(src, dst, send, recv, device):
        return pltpu.make_async_remote_copy(
            src_ref=src, dst_ref=dst, send_sem=send, recv_sem=recv, device_id=device, device_id_type=MESH
        )

    barrier = pltpu.get_barrier_semaphore()
    for i in range(1, leafs):
        pl.semaphore_signal(barrier, inc=1, device_id={"leaf": lax.rem(leaf + i, leafs)}, device_id_type=MESH)
    for i in range(1, fronts):
        pl.semaphore_signal(barrier, inc=1, device_id=to(lax.rem(me + i, fronts)), device_id_type=MESH)
    pl.semaphore_wait(barrier, leafs + fronts - 2)

    def child_copies(i):
        peer = lax.rem(leaf + i, leafs)
        device = {"leaf": peer}
        return (
            remote(child.at[peer], child_in.at[i], child_send.at[i], child_recv.at[i], device),
            remote(codes.at[peer], codes_in.at[i], code_send.at[i], code_recv.at[i], device),
        )

    for i in range(1, leafs):
        for copy in child_copies(i):
            copy.start()
    child_in[0] = child[leaf]
    codes_in[0] = codes[leaf]
    for i in range(1, leafs):
        for copy in child_copies(i):
            copy.wait()

    def assemble(column, carry):
        lanes = pl.ds(pl.multiple_of(column * BLOCK, BLOCK), BLOCK)
        for r in range(row_blocks):
            total = front[r * BLOCK : (r + 1) * BLOCK, lanes]
            place = r * col_blocks + column
            for i in range(leafs):
                for j in range(slots):
                    hit = codes_in[i, j : j + 1, :] == place
                    total = total + jnp.where(hit, child_in[i, j], 0.0)
            mine[column, r * BLOCK : (r + 1) * BLOCK, :] = total
        return carry

    lax.fori_loop(0, col_blocks, assemble, 0)

    def owner_rows(owner):
        return pl.ds(owner * rows, rows)

    def last_column(owner):
        return min(STEPS, (owner + 1) * row_blocks)

    def top_copy(owner, column, target):
        place = top.at[column, owner_rows(owner)]
        return remote(mine.at[column], place, top_send.at[column, target], top_recv.at[owner, column], to(target))

    def relay_copy(owner, column):
        place = top.at[column, owner_rows(owner)]
        target = lax.rem(me + slab, fronts)
        return remote(place, place, relay_send.at[owner, column], top_recv.at[owner, column], to(target))

    def owners(column):
        return [o for o in range(tops) if column < last_column(o)]

    for column in range(STEPS):
        for owner in owners(column):

            @pl.when(me == owner)
            def _():
                for target in range(3 * slab):
                    if target != owner:
                        top_copy(owner, column, target).start()
                top[column, owner * rows : (owner + 1) * rows, :] = mine[column]

    def arrive(column):
        for owner in owners(column):

            @pl.when(me != owner)
            def _():
                top_copy(owner, column, 0).wait_recv()

            @pl.when(depth == 2)
            def _():
                relay_copy(owner, column).start()

    def far_copy(column, target):
        return remote(
            own_w.at[column], far_w.at[me - tops, column], far_send.at[column, target],
            far_recv.at[me - tops, column], to(tops + target),
        )

    arrive(0)
    row_id = lax.broadcasted_iota(jnp.int32, (BLOCK, BLOCK), 0)
    col_id = lax.broadcasted_iota(jnp.int32, (BLOCK, BLOCK), 1)
    for step in range(STEPS):
        begin, end = step * BLOCK, (step + 1) * BLOCK
        lanes = slice(begin, end)
        current = jnp.concatenate([top[step, begin:, :], rhs[:, lanes], mine[step]], axis=0)
        if step:
            past = slice(0, begin)
            current = current - dot3(
                (high[begin:, past], low[begin:, past]), (high[begin:end, past], low[begin:end, past])
            )
        square = current[:BLOCK]
        work[:, :BLOCK] = jnp.where(row_id >= col_id, square, 0.0) + jnp.where(row_id > col_id, square, 0.0).T
        work[:, BLOCK:] = jnp.where(row_id == col_id, 1.0, 0.0)
        block_factor(work)
        if step + 1 < STEPS:
            arrive(step + 1)
        upper = work[:, :BLOCK]
        on_diag = jnp.where(row_id == col_id, upper, 0.0)
        pivots = jnp.sum(on_diag, axis=0, keepdims=True)
        pivots_down = jnp.sum(on_diag, axis=1, keepdims=True)
        value = dot3(split(current[BLOCK:]), split(work[:, BLOCK:]))
        weighted = value * lax.rsqrt(pivots)
        high[end:, lanes], low[end:, lanes] = split(weighted)
        unit = value / pivots
        if step:
            lead[begin - BLOCK : begin, :] = jnp.zeros((BLOCK, BLOCK), jnp.float32)
        lead[begin:end, :] = on_diag + jnp.where(col_id > row_id, upper / pivots_down, 0.0).T
        inside = PIVOTS - end
        if inside:
            lead[end:, :] = unit[:inside]
        elim[:, lanes] = value[inside : inside + shots]

        @pl.when(here)
        def _():
            out[:, lanes] = lead[pl.ds(pl.multiple_of(me * rows, rows), rows), :]

        @pl.when(below)
        def _():
            out[:, lanes] = unit[inside + shots :]
            own_w[step] = weighted[inside + shots :]
            for target in range(1, fronts - tops):

                @pl.when(me < tops + target)
                def _():
                    far_copy(step, target).start()

    def tail_copy(source, target_step):
        target = lax.rem(source + target_step, fronts)
        return remote(
            tail_out, tail_in.at[source - tops], tail_send.at[target_step], tail_recv.at[source - tops], to(target)
        )

    first = PIVOTS + shots

    @pl.when(below)
    def _():
        lanes = pl.ds(pl.multiple_of(PIVOTS + (me - tops) * rows, BLOCK), rows)
        shot = (high[PIVOTS:first, :], low[PIVOTS:first, :])
        tail = rhs[:, lanes] - dot3(shot, (high[first:, :], low[first:, :]))
        tail_out[...] = tail
        for i in range(1, fronts):
            tail_copy(me, i).start()
        tail_in[me - tops] = tail

    for part in range(fronts - tops):
        source = tops + part
        lanes = slice(PIVOTS + part * rows, PIVOTS + (part + 1) * rows)
        base = STEPS + part * row_blocks

        def pieces():
            return jnp.concatenate([mine[base + r] for r in range(row_blocks)], axis=1)

        @pl.when(me < source)
        def _():
            out[:, lanes] = jnp.zeros((rows, rows), jnp.float32)

        @pl.when(me == source)
        def _():
            own = (high[first:, :], low[first:, :])
            result = pieces() - dot3(own, own)
            r = lax.broadcasted_iota(jnp.int32, result.shape, 0)
            c = lax.broadcasted_iota(jnp.int32, result.shape, 1)
            out[:, lanes] = jnp.where(r >= c, result, 0.0)

        @pl.when(me > source)
        def _():
            for step in range(STEPS):
                remote(
                    own_w.at[step], far_w.at[part, step], far_send.at[step, 0], far_recv.at[part, step], to(source)
                ).wait_recv()
            other = jnp.concatenate([far_w[part, step] for step in range(STEPS)], axis=1)
            out[:, lanes] = pieces() - dot3((high[first:, :], low[first:, :]), split(other))

    for part in range(fronts - tops):

        @pl.when(me != tops + part)
        def _():
            remote(
                tail_out, tail_in.at[part], tail_send.at[0], tail_recv.at[part], to(tops + part)
            ).wait_recv()

        elim[:, PIVOTS + part * rows : PIVOTS + (part + 1) * rows] = tail_in[part]

    for column in range(STEPS):
        for owner in owners(column):

            @pl.when(me == owner)
            def _():
                for target in range(3 * slab):
                    if target != owner:
                        top_copy(owner, column, target).wait_send()

            @pl.when(depth == 2)
            def _():
                relay_copy(owner, column).wait_send()

        for target in range(1, fronts - tops):

            @pl.when(below & (me < tops + target))
            def _():
                far_copy(column, target).wait_send()

    @pl.when(below)
    def _():
        for i in range(1, fronts):
            tail_copy(me, i).wait_send()


def local(front_matrix, child_blocks, child_target, child_count, shot_rhs):
    _, rows, order = front_matrix.shape
    leafs, fronts = lax.axis_size("leaf"), lax.axis_size("front")
    slots = child_blocks.shape[2]
    shots = shot_rhs.shape[1]
    slot_ids = lax.broadcasted_iota(jnp.int32, child_target.shape, 2)
    live = jnp.where(slot_ids < child_count[:, :, None], child_target, -1)[0]
    codes = jnp.pad(live, ((0, 0), (0, 8 - slots)), constant_values=-1)
    codes = jnp.broadcast_to(codes[:, :, None], (leafs, 8, BLOCK))
    tops = PIVOTS // rows
    parts = fronts - tops
    stack = PIVOTS + shots + rows
    f32 = jnp.float32
    dma = pltpu.SemaphoreType.DMA
    vmem = pl.BlockSpec(memory_space=pltpu.VMEM)
    factored, eliminated = pl.pallas_call(
        functools.partial(kernel, leafs, fronts),
        out_shape=(jax.ShapeDtypeStruct((rows, order), f32), jax.ShapeDtypeStruct((shots, order), f32)),
        in_specs=[vmem] * 4,
        out_specs=(vmem, vmem),
        scratch_shapes=[
            pltpu.VMEM((leafs, slots, BLOCK, BLOCK), f32),
            pltpu.VMEM((leafs, 8, BLOCK), jnp.int32),
            pltpu.VMEM((order // BLOCK, rows, BLOCK), f32),
            pltpu.VMEM((STEPS, PIVOTS, BLOCK), f32),
            pltpu.VMEM((stack, PIVOTS), jnp.bfloat16),
            pltpu.VMEM((stack, PIVOTS), jnp.bfloat16),
            pltpu.VMEM((PIVOTS, BLOCK), f32),
            pltpu.VMEM((BLOCK, 2 * BLOCK), f32),
            pltpu.VMEM((STEPS, rows, BLOCK), f32),
            pltpu.VMEM((parts, STEPS, rows, BLOCK), f32),
            pltpu.VMEM((shots, rows), f32),
            pltpu.VMEM((parts, shots, rows), f32),
            dma((leafs,)),
            dma((leafs,)),
            dma((leafs,)),
            dma((leafs,)),
            dma((STEPS, fronts)),
            dma((tops, STEPS)),
            dma((tops, STEPS)),
            dma((STEPS, parts)),
            dma((parts, STEPS)),
            dma((fronts,)),
            dma((parts,)),
        ],
        compiler_params=pltpu.CompilerParams(
            collective_id=0, has_side_effects=True, vmem_limit_bytes=56 * 1024 * 1024
        ),
        cost_estimate=pl.CostEstimate(
            flops=6 * stack * PIVOTS * PIVOTS, bytes_accessed=8 * rows * order, transcendentals=0
        ),
    )(front_matrix[0], child_blocks[0], codes, shot_rhs[0])
    return factored[None], eliminated[None]


def solution(mesh):
    return jax.shard_map(
        local,
        mesh=mesh,
        in_specs=(
            P("leaf", "front", None),
            P(("leaf", "front"), None, None, None, None),
            P(("leaf", "front"), None, None),
            P(("leaf", "front"), None),
            P("leaf", None, None),
        ),
        out_specs=(P("leaf", "front", None), P("leaf", None, None)),
        check_vma=False,
    )
```

```python
import functools

import jax
import jax.numpy as jnp
from jax import lax
from jax.experimental import pallas as pl
from jax.experimental.pallas import tpu as pltpu
from jax.sharding import PartitionSpec as P

BLOCK = 128
PIVOTS = 1024
STEPS = PIVOTS // BLOCK
PANEL = 8
MESH = pl.DeviceIdType.MESH
NT = (((1,), (1,)), ((), ()))
TN = (((0,), (0,)), ((), ()))


def split(value):
    high = value.astype(jnp.bfloat16)
    low = (value - high.astype(jnp.float32)).astype(jnp.bfloat16)
    return high, low


def dot3(left, right):
    dot = functools.partial(lax.dot_general, dimension_numbers=NT, preferred_element_type=jnp.float32)
    return dot(left[0], right[0]) + (dot(left[0], right[1]) + dot(left[1], right[0]))


def wide(value):
    return jnp.broadcast_to(value, (PANEL, BLOCK))


def panel_factor(left, right, start):
    columns = [wide(left[:, start + j : start + j + 1]) for j in range(PANEL)]
    entry = [[wide(columns[j][i : i + 1]) for j in range(i + 1)] for i in range(PANEL)]
    lower = [[None] * PANEL for _ in range(PANEL)]
    reciprocal = []
    for j in range(PANEL):
        reciprocal.append(1.0 / entry[j][j])
        for i in range(j + 1, PANEL):
            lower[i][j] = entry[i][j] * reciprocal[j]
        for i in range(j + 1, PANEL):
            for k in range(j + 1, i + 1):
                entry[i][k] = entry[i][k] - lower[i][j] * entry[k][j]
    rows = lax.broadcasted_iota(jnp.int32, (PANEL, BLOCK), 0)
    inverse = [[None] * PANEL for _ in range(PANEL)]
    new_left, new_right = left, right
    for j in range(PANEL - 1):
        column = jnp.zeros((PANEL, BLOCK), jnp.float32)
        for i in range(j + 1, PANEL):
            total = lower[i][j]
            for k in range(j + 1, i):
                total = total + lower[i][k] * inverse[k][j]
            inverse[i][j] = -total
            column = jnp.where(rows == i, -total, column)
        new_left = new_left + column * left[j : j + 1]
        new_right = new_right + column * right[j : j + 1]
    return new_left, new_right, inverse, reciprocal


def halves(value, order):
    high = value.astype(jnp.bfloat16).astype(jnp.float32)
    parts = (high, value - high)
    return jnp.concatenate([parts[i] for i in order], axis=0).astype(jnp.bfloat16)


def block_factor(work):
    count = BLOCK // PANEL
    left = [work[i * PANEL : (i + 1) * PANEL, :BLOCK] for i in range(count)]
    right = [work[i * PANEL : (i + 1) * PANEL, BLOCK:] for i in range(count)]
    rows = lax.broadcasted_iota(jnp.int32, (PANEL, BLOCK), 0)
    for b in range(count):
        start = b * PANEL
        done_left, done_right, inverse, reciprocal = panel_factor(left[b], right[b], start)
        work[start : start + PANEL, :BLOCK] = done_left
        work[start : start + PANEL, BLOCK:] = done_right
        if b + 1 < count:
            columns = [wide(left[b + 1][:, start + j : start + j + 1]) for j in range(PANEL)]
            for j in range(PANEL):
                factor = columns[j]
                for k in range(j):
                    factor = factor + inverse[j][k] * columns[k]
                factor = factor * reciprocal[j]
                left[b + 1] = left[b + 1] - factor * done_left[j : j + 1]
                right[b + 1] = right[b + 1] - factor * done_right[j : j + 1]
        if b + 2 < count:
            scale = reciprocal[0]
            for j in range(1, PANEL):
                scale = jnp.where(rows == j, reciprocal[j], scale)
            both = jnp.concatenate([done_left, done_right], axis=1)
            update = lax.dot_general(
                halves(done_left * scale, (0, 0, 1)), halves(both, (0, 1, 0)), TN,
                preferred_element_type=jnp.float32,
            )
            for i in range(b + 2, count):
                left[i] = left[i] - update[i * PANEL : (i + 1) * PANEL, :BLOCK]
                right[i] = right[i] - update[i * PANEL : (i + 1) * PANEL, BLOCK:]


def kernel(
    leafs, fronts, front, child, codes, rhs, out, elim,
    child_in, codes_in, mine, top, high, low, lead, work, column_now, own_w, far_w, tail_out, tail_in,
    child_send, child_recv, code_send, code_recv, top_send, top_recv, relay_send,
    far_send, far_recv, tail_send, tail_recv,
):
    rows, order = front.shape
    shots = rhs.shape[0]
    slots = child.shape[1]
    col_blocks = order // BLOCK
    row_blocks = rows // BLOCK
    tops = PIVOTS // rows
    slab = fronts // 4
    me = lax.axis_index("front")
    leaf = lax.axis_index("leaf")
    depth = me // slab
    here = me < tops
    below = me >= tops

    def to(front_id):
        return {"front": front_id}

    def remote(src, dst, send, recv, device):
        return pltpu.make_async_remote_copy(
            src_ref=src, dst_ref=dst, send_sem=send, recv_sem=recv, device_id=device, device_id_type=MESH
        )

    barrier = pltpu.get_barrier_semaphore()
    for i in range(1, leafs):
        pl.semaphore_signal(barrier, inc=1, device_id={"leaf": lax.rem(leaf + i, leafs)}, device_id_type=MESH)
    for i in range(1, fronts):
        pl.semaphore_signal(barrier, inc=1, device_id=to(lax.rem(me + i, fronts)), device_id_type=MESH)
    pl.semaphore_wait(barrier, leafs + fronts - 2)

    def child_copies(i):
        peer = lax.rem(leaf + i, leafs)
        device = {"leaf": peer}
        return (
            remote(child.at[peer], child_in.at[i], child_send.at[i], child_recv.at[i], device),
            remote(codes.at[peer], codes_in.at[i], code_send.at[i], code_recv.at[i], device),
        )

    for i in range(1, leafs):
        for copy in child_copies(i):
            copy.start()
    child_in[0] = child[leaf]
    codes_in[0] = codes[leaf]
    for i in range(1, leafs):
        for copy in child_copies(i):
            copy.wait()

    def assemble(column, carry):
        lanes = pl.ds(pl.multiple_of(column * BLOCK, BLOCK), BLOCK)
        for r in range(row_blocks):
            total = front[r * BLOCK : (r + 1) * BLOCK, lanes]
            place = r * col_blocks + column
            for i in range(leafs):
                for j in range(slots):
                    hit = codes_in[i, j : j + 1, :] == place
                    total = total + jnp.where(hit, child_in[i, j], 0.0)
            mine[column, r * BLOCK : (r + 1) * BLOCK, :] = total
        return carry

    lax.fori_loop(0, col_blocks, assemble, 0)

    def owner_rows(owner):
        return pl.ds(owner * rows, rows)

    def last_column(owner):
        return min(STEPS, (owner + 1) * row_blocks)

    def top_copy(owner, column, target):
        place = top.at[column, owner_rows(owner)]
        return remote(mine.at[column], place, top_send.at[column, target], top_recv.at[owner, column], to(target))

    def relay_copy(owner, column):
        place = top.at[column, owner_rows(owner)]
        target = lax.rem(me + slab, fronts)
        return remote(place, place, relay_send.at[owner, column], top_recv.at[owner, column], to(target))

    def owners(column):
        return [o for o in range(tops) if column < last_column(o)]

    for column in range(STEPS):
        for owner in owners(column):

            @pl.when(me == owner)
            def _():
                for target in range(3 * slab):
                    if target != owner:
                        top_copy(owner, column, target).start()
                top[column, owner * rows : (owner + 1) * rows, :] = mine[column]

    def arrive(column):
        for owner in owners(column):

            @pl.when(me != owner)
            def _():
                top_copy(owner, column, 0).wait_recv()

            @pl.when(depth == 2)
            def _():
                relay_copy(owner, column).start()

    def far_copy(column, target):
        return remote(
            own_w.at[column], far_w.at[me - tops, column], far_send.at[column, target],
            far_recv.at[me - tops, column], to(tops + target),
        )

    arrive(0)
    row_id = lax.broadcasted_iota(jnp.int32, (BLOCK, BLOCK), 0)
    col_id = lax.broadcasted_iota(jnp.int32, (BLOCK, BLOCK), 1)
    def before(step):
        begin, end = step * BLOCK, (step + 1) * BLOCK
        lanes = slice(begin, end)
        current = jnp.concatenate([top[step, begin:, :], rhs[:, lanes], mine[step]], axis=0)
        if step:
            past = slice(0, begin)
            current = current - dot3(
                (high[begin:, past], low[begin:, past]), (high[begin:end, past], low[begin:end, past])
            )
        square = current[:BLOCK]
        work[:, :BLOCK] = jnp.where(row_id >= col_id, square, 0.0) + jnp.where(row_id > col_id, square, 0.0).T
        work[:, BLOCK:] = jnp.where(row_id == col_id, 1.0, 0.0)
        column_now[end:, :] = current[BLOCK:]

    def after(step):
        begin, end = step * BLOCK, (step + 1) * BLOCK
        lanes = slice(begin, end)
        if step + 1 < STEPS:
            arrive(step + 1)
        upper = work[:, :BLOCK]
        on_diag = jnp.where(row_id == col_id, upper, 0.0)
        pivots = jnp.sum(on_diag, axis=0, keepdims=True)
        pivots_down = jnp.sum(on_diag, axis=1, keepdims=True)
        value = dot3(split(column_now[end:, :]), split(work[:, BLOCK:]))
        weighted = value * lax.rsqrt(pivots)
        high[end:, lanes], low[end:, lanes] = split(weighted)
        unit = value * (1.0 / pivots)
        if step:
            lead[begin - BLOCK : begin, :] = jnp.zeros((BLOCK, BLOCK), jnp.float32)
        lead[begin:end, :] = on_diag + jnp.where(col_id > row_id, upper / pivots_down, 0.0).T
        inside = PIVOTS - end
        if inside:
            lead[end:, :] = unit[:inside]
        elim[:, lanes] = value[inside : inside + shots]

        @pl.when(here)
        def _():
            out[:, lanes] = lead[pl.ds(pl.multiple_of(me * rows, rows), rows), :]

        @pl.when(below)
        def _():
            out[:, lanes] = unit[inside + shots :]
            own_w[step] = weighted[inside + shots :]
            for target in range(1, fronts - tops):

                @pl.when(me < tops + target)
                def _():
                    far_copy(step, target).start()

    def one_step(index, carry):
        for step in range(STEPS):
            pl.when(index == step)(functools.partial(before, step))
        block_factor(work)
        for step in range(STEPS):
            pl.when(index == step)(functools.partial(after, step))
        return carry

    lax.fori_loop(0, STEPS, one_step, 0)

    def tail_copy(source, target_step):
        target = lax.rem(source + target_step, fronts)
        return remote(
            tail_out, tail_in.at[source - tops], tail_send.at[target_step], tail_recv.at[source - tops], to(target)
        )

    first = PIVOTS + shots

    @pl.when(below)
    def _():
        lanes = pl.ds(pl.multiple_of(PIVOTS + (me - tops) * rows, BLOCK), rows)
        shot = (high[PIVOTS:first, :], low[PIVOTS:first, :])
        tail = rhs[:, lanes] - dot3(shot, (high[first:, :], low[first:, :]))
        tail_out[...] = tail
        for i in range(1, fronts):
            tail_copy(me, i).start()
        tail_in[me - tops] = tail

    for part in range(fronts - tops):
        source = tops + part
        lanes = slice(PIVOTS + part * rows, PIVOTS + (part + 1) * rows)
        base = STEPS + part * row_blocks

        def pieces():
            return jnp.concatenate([mine[base + r] for r in range(row_blocks)], axis=1)

        @pl.when(me < source)
        def _():
            out[:, lanes] = jnp.zeros((rows, rows), jnp.float32)

        @pl.when(me == source)
        def _():
            own = (high[first:, :], low[first:, :])
            result = pieces() - dot3(own, own)
            r = lax.broadcasted_iota(jnp.int32, result.shape, 0)
            c = lax.broadcasted_iota(jnp.int32, result.shape, 1)
            out[:, lanes] = jnp.where(r >= c, result, 0.0)

        @pl.when(me > source)
        def _():
            for step in range(STEPS):
                remote(
                    own_w.at[step], far_w.at[part, step], far_send.at[step, 0], far_recv.at[part, step], to(source)
                ).wait_recv()
            other = jnp.concatenate([far_w[part, step] for step in range(STEPS)], axis=1)
            out[:, lanes] = pieces() - dot3((high[first:, :], low[first:, :]), split(other))

    for part in range(fronts - tops):

        @pl.when(me != tops + part)
        def _():
            remote(
                tail_out, tail_in.at[part], tail_send.at[0], tail_recv.at[part], to(tops + part)
            ).wait_recv()

        elim[:, PIVOTS + part * rows : PIVOTS + (part + 1) * rows] = tail_in[part]

    for column in range(STEPS):
        for owner in owners(column):

            @pl.when(me == owner)
            def _():
                for target in range(3 * slab):
                    if target != owner:
                        top_copy(owner, column, target).wait_send()

            @pl.when(depth == 2)
            def _():
                relay_copy(owner, column).wait_send()

        for target in range(1, fronts - tops):

            @pl.when(below & (me < tops + target))
            def _():
                far_copy(column, target).wait_send()

    @pl.when(below)
    def _():
        for i in range(1, fronts):
            tail_copy(me, i).wait_send()


def local(front_matrix, child_blocks, child_target, child_count, shot_rhs):
    _, rows, order = front_matrix.shape
    leafs, fronts = lax.axis_size("leaf"), lax.axis_size("front")
    slots = child_blocks.shape[2]
    shots = shot_rhs.shape[1]
    slot_ids = lax.broadcasted_iota(jnp.int32, child_target.shape, 2)
    live = jnp.where(slot_ids < child_count[:, :, None], child_target, -1)[0]
    codes = jnp.pad(live, ((0, 0), (0, 8 - slots)), constant_values=-1)
    codes = jnp.broadcast_to(codes[:, :, None], (leafs, 8, BLOCK))
    tops = PIVOTS // rows
    parts = fronts - tops
    stack = PIVOTS + shots + rows
    f32 = jnp.float32
    dma = pltpu.SemaphoreType.DMA
    vmem = pl.BlockSpec(memory_space=pltpu.VMEM)
    factored, eliminated = pl.pallas_call(
        functools.partial(kernel, leafs, fronts),
        out_shape=(jax.ShapeDtypeStruct((rows, order), f32), jax.ShapeDtypeStruct((shots, order), f32)),
        in_specs=[vmem] * 4,
        out_specs=(vmem, vmem),
        scratch_shapes=[
            pltpu.VMEM((leafs, slots, BLOCK, BLOCK), f32),
            pltpu.VMEM((leafs, 8, BLOCK), jnp.int32),
            pltpu.VMEM((order // BLOCK, rows, BLOCK), f32),
            pltpu.VMEM((STEPS, PIVOTS, BLOCK), f32),
            pltpu.VMEM((stack, PIVOTS), jnp.bfloat16),
            pltpu.VMEM((stack, PIVOTS), jnp.bfloat16),
            pltpu.VMEM((PIVOTS, BLOCK), f32),
            pltpu.VMEM((BLOCK, 2 * BLOCK), f32),
            pltpu.VMEM((stack, BLOCK), f32),
            pltpu.VMEM((STEPS, rows, BLOCK), f32),
            pltpu.VMEM((parts, STEPS, rows, BLOCK), f32),
            pltpu.VMEM((shots, rows), f32),
            pltpu.VMEM((parts, shots, rows), f32),
            dma((leafs,)),
            dma((leafs,)),
            dma((leafs,)),
            dma((leafs,)),
            dma((STEPS, fronts)),
            dma((tops, STEPS)),
            dma((tops, STEPS)),
            dma((STEPS, parts)),
            dma((parts, STEPS)),
            dma((fronts,)),
            dma((parts,)),
        ],
        compiler_params=pltpu.CompilerParams(
            collective_id=0, has_side_effects=True, vmem_limit_bytes=56 * 1024 * 1024
        ),
        cost_estimate=pl.CostEstimate(
            flops=6 * stack * PIVOTS * PIVOTS, bytes_accessed=8 * rows * order, transcendentals=0
        ),
    )(front_matrix[0], child_blocks[0], codes, shot_rhs[0])
    return factored[None], eliminated[None]


def solution(mesh):
    return jax.shard_map(
        local,
        mesh=mesh,
        in_specs=(
            P("leaf", "front", None),
            P(("leaf", "front"), None, None, None, None),
            P(("leaf", "front"), None, None),
            P(("leaf", "front"), None),
            P("leaf", None, None),
        ),
        out_specs=(P("leaf", "front", None), P("leaf", None, None)),
        check_vma=False,
    )
```
